32 devices in a mesh: grp: 8 (over y, x, core), sub: 4 (over z).
Axes of the slice: x: 2, y: 2, z: 4, core: 2. Of those that a mesh axis runs over, the one named last changes fastest.
Arguments:
- loads: bfloat16 [8, 4, 16, 1536], P('grp', 'sub'), may hold values from -6 to 6
- boundary_values: float32 [16, 6144], replicated, may hold values from -6 to 6
- dirichlet_ids: int32 [8, 4, 3, 128], P('grp', 'sub'), may hold values from 0 to 6143
- dirichlet_coupling: bfloat16 [8, 4, 3, 512, 128], P('grp', 'sub'), may hold values from -0.5 to 0.5
- local_inverse: bfloat16 [8, 4, 3, 512, 512], P('grp', 'sub'), as said below
- local_schur: bfloat16 [8, 4, 3, 512, 512], P('grp', 'sub')
- corner_coupling: bfloat16 [8, 4, 3, 24, 512], P('grp', 'sub'), may hold values from -0.25 to 0.25
- corner_ids: int32 [8, 4, 3, 24], P('grp', 'sub'), may hold values from 0 to 767
- coarse_inverse: bfloat16 [768, 768], P(('grp', 'sub')), as said below
- row_counts: int32 [8, 4, 6], P('grp', 'sub'), may hold values from 0 to 256, as said below
- slot_of: int32 [8, 4, 1536], P('grp', 'sub'), may hold values from 0 to 1535, each once within a row
Outputs:
- multipliers: float32 [8, 4, 16, 1536], P('grp', 'sub')
- residual: float32 [8, 4, 16, 1536], P('grp', 'sub')
The draws below stay inside these ranges and needn't reach their ends.
Inputs may be any that keep to these rules, and one draw needn't show every extreme that they name: row_counts[g, s, p] for p < 4 equals row_counts[g, p, s], is 0 for p = s and lies in 1 to 256 otherwise; every device reaches 256 with some peer. Column 4 of device (g, s) equals column 5 of device (g - 1, s), lies in 1 to 256, reaches 256 on some device of every slab boundary, and is 0 in the first slab; column 5 is 0 in the last slab. coarse_inverse is symmetric and positive definite. local_inverse and local_schur are symmetric and positive definite.
All inputs are finite; a program needn't handle non-finite values.
Results may differ from the reference program's by a relative error of at most 0.012.
Values may be sent and summed in bfloat16 or wider, within the bound.
A program may use at most 64 MiB of HBM per device.

```python
import math
import jax
import jax.numpy as jnp
from jax import lax

IFACE = 512
SUBS_DEV = 3
LOADS = 16
CORNERS = 24
FIXED_DOFS = 128
BOUNDARY = 6144
SLAB_ROWS = 256
ITERS = 2
SLOTS = 1536
PEER_ROWS = 256
COARSE = 768
N_GRP = 8
N_SUB = 4


def symmetric_block(key, lead, order, scale):
    first, second = jax.random.split(key)
    shape = lead + (order, order)
    base = jax.random.normal(first, shape, jnp.float32)
    mixed = (base + jnp.swapaxes(base, -1, -2)) * (scale / math.sqrt(2.0 * order))
    diagonal = jnp.exp(jax.random.uniform(second, lead + (order, 1), jnp.float32, 0.0, math.log(4.0)))
    identity = jnp.eye(order, dtype=jnp.float32)
    return mixed * (1.0 - identity) + identity * diagonal


def draw_local_inverse(key, part):
    return symmetric_block(jax.random.fold_in(key, 11), (N_GRP, N_SUB, SUBS_DEV), IFACE, 0.45).astype(jnp.bfloat16)


def draw_local_schur(key, part):
    return symmetric_block(jax.random.fold_in(key, 23), (N_GRP, N_SUB, SUBS_DEV), IFACE, 0.45).astype(jnp.bfloat16)


def draw_coarse_inverse(key, part):
    return symmetric_block(jax.random.fold_in(key, 37), (), COARSE, 0.45).astype(jnp.bfloat16)


def draw_row_counts(key, part):
    first, second = jax.random.split(jax.random.fold_in(key, 41))
    paired = jax.random.randint(first, (N_GRP, N_SUB, N_SUB), max(1, PEER_ROWS // 3), PEER_ROWS + 1)
    index = jnp.arange(N_SUB, dtype=jnp.int32)
    upper_half = (index[:, None] < index[None, :])[None]
    mirror = jnp.where(upper_half, paired, jnp.swapaxes(paired, 1, 2))
    mates = (index[:, None] ^ 1 == index[None, :])[None]
    mirror = jnp.where(mates, PEER_ROWS, mirror)
    mirror = jnp.where((index[:, None] == index[None, :])[None], 0, mirror)
    slab = jax.random.randint(second, (N_GRP, N_SUB), max(1, SLAB_ROWS // 3), SLAB_ROWS + 1)
    slab = jnp.where(index[None, :] == 0, SLAB_ROWS, slab)
    groups = jnp.arange(N_GRP, dtype=jnp.int32)[:, None]
    above = jnp.where(groups < N_GRP - 1, slab, 0)
    below = jnp.concatenate([jnp.zeros((1, N_SUB), jnp.int32), above[:-1]], axis=0)
    return jnp.concatenate([mirror, below[:, :, None], above[:, :, None]], axis=2).astype(jnp.int32)


def plant(values, own_key, low, high):
    spot = [jax.random.randint(jax.random.fold_in(own_key, axis), (), 0, length) for axis, length in enumerate(values.shape)]
    longest = values.shape.index(max(values.shape))
    beside = spot[:longest] + [(spot[longest] + 1) % values.shape[longest]] + spot[longest + 1:]
    return values.at[tuple(spot)].set(low).at[tuple(beside)].set(high)


def block_levels(key, shape, pieces, least, high):
    loudness = 1.0
    for dim, blocks in pieces:
        steps = jax.random.uniform(jax.random.fold_in(jax.random.fold_in(key, 6), dim), (blocks,), jnp.float32, least / len(pieces), high / len(pieces))
        loudness = loudness * jnp.repeat(jnp.exp(steps), shape[dim] // blocks).reshape((-1,) + (1,) * (len(shape) - 1 - dim))
    return loudness


def gaussian(own_key, shape, width, limit, cuts=(), held_as=jnp.bfloat16):
    entries = width * jax.random.normal(own_key, shape, jnp.float32)
    if cuts:
        entries = entries * block_levels(own_key, shape, cuts, -0.22, 0.18)
    return jnp.clip(entries, -limit, limit).astype(held_as)


def setup_inputs(seed: int = 0) -> dict:
    arg_keys = jax.random.split(jax.random.key(seed), 12)
    loads = gaussian(arg_keys[0], (N_GRP, N_SUB, LOADS, SLOTS), 1.0, 6.0, ((0, 8), (1, 4)))
    boundary_values = gaussian(arg_keys[1], (LOADS, BOUNDARY), 1.0, 6.0, (), jnp.float32)
    dirichlet_ids = plant(jax.random.randint(arg_keys[2], (N_GRP, N_SUB, SUBS_DEV, FIXED_DOFS), 0, BOUNDARY), jax.random.fold_in(arg_keys[2], 1), 0, BOUNDARY - 1).astype(jnp.int32)
    dirichlet_coupling = gaussian(arg_keys[3], (N_GRP, N_SUB, SUBS_DEV, IFACE, FIXED_DOFS), FIXED_DOFS ** -0.5, 0.5, ((0, 8), (1, 4)))
    local_inverse = draw_local_inverse(jax.random.fold_in(arg_keys[11], 71), 0)
    local_schur = draw_local_schur(jax.random.fold_in(arg_keys[11], 71), 0)
    corner_coupling = gaussian(arg_keys[6], (N_GRP, N_SUB, SUBS_DEV, CORNERS, IFACE), IFACE ** -0.5, 0.25, ((0, 8), (1, 4)))
    corner_ids = plant(jax.random.randint(arg_keys[7], (N_GRP, N_SUB, SUBS_DEV, CORNERS), 0, COARSE), jax.random.fold_in(arg_keys[7], 1), 0, COARSE - 1).astype(jnp.int32)
    coarse_inverse = draw_coarse_inverse(jax.random.fold_in(arg_keys[11], 71), 0)
    row_counts = draw_row_counts(jax.random.fold_in(arg_keys[11], 71), 0)
    slot_of = jax.vmap(lambda own: jax.random.permutation(own, SLOTS))(jax.random.split(arg_keys[10], N_GRP * N_SUB)).reshape((N_GRP, N_SUB, SLOTS)).astype(jnp.int32)
    return {"loads": loads, "boundary_values": boundary_values, "dirichlet_ids": dirichlet_ids, "dirichlet_coupling": dirichlet_coupling, "local_inverse": local_inverse, "local_schur": local_schur, "corner_coupling": corner_coupling, "corner_ids": corner_ids, "coarse_inverse": coarse_inverse, "row_counts": row_counts, "slot_of": slot_of}


def slot_tables(row_counts, slot_of):
    length = SUBS_DEV * IFACE
    within = N_SUB * PEER_ROWS
    positions = jnp.arange(length, dtype=jnp.int32)
    inverse = jax.vmap(jax.vmap(lambda order: jnp.zeros(length, jnp.int32).at[order].set(positions)))(slot_of)
    column = jnp.where(positions < within, positions // PEER_ROWS, N_SUB + (positions - within) // SLAB_ROWS).astype(jnp.int32)
    offset = jnp.where(positions < within, positions % PEER_ROWS, (positions - within) % SLAB_ROWS).astype(jnp.int32)
    counts = jnp.take(row_counts, column, axis=2)
    canon_live = (offset[None, None, :] < counts).astype(jnp.float32)
    live = jnp.take_along_axis(canon_live, inverse, axis=2)
    return inverse, live


def partner(values, slot_of, inverse):
    within = N_SUB * PEER_ROWS
    canon = jnp.take_along_axis(values, jnp.broadcast_to(slot_of[:, :, None, :], values.shape), axis=3)
    inner_part = canon[..., :within].reshape(N_GRP, N_SUB, LOADS, N_SUB, PEER_ROWS)
    paired = jnp.transpose(inner_part, (0, 3, 2, 1, 4)).reshape(N_GRP, N_SUB, LOADS, within)
    lower_side = canon[..., within:within + SLAB_ROWS]
    upper_side = canon[..., within + SLAB_ROWS:]
    from_below = jnp.concatenate([jnp.zeros_like(upper_side[:1]), upper_side[:-1]], axis=0)
    from_above = jnp.concatenate([lower_side[1:], jnp.zeros_like(lower_side[:1])], axis=0)
    joined = jnp.concatenate([paired, from_below, from_above], axis=3)
    return jnp.take_along_axis(joined, jnp.broadcast_to(inverse[:, :, None, :], values.shape), axis=3)


def block_apply(matrices, field_b):
    blocks = field_b.reshape(N_GRP * N_SUB, LOADS, SUBS_DEV, IFACE)

    def one_device(pair):
        matrix, vector = pair
        return jnp.einsum('anm,ram->ran', matrix.astype(jnp.float32), vector.astype(jnp.float32))

    result = lax.map(one_device, (matrices.reshape(N_GRP * N_SUB, SUBS_DEV, IFACE, IFACE), blocks))
    return result.reshape(N_GRP, N_SUB, LOADS, SUBS_DEV * IFACE)


def apply_tilde(field_b, local_inverse, corner_coupling, corner_ids, coarse_inverse):
    local_part = block_apply(local_inverse, field_b)
    blocks = field_b.reshape(N_GRP, N_SUB, LOADS, SUBS_DEV, IFACE).astype(jnp.float32)
    coupling = corner_coupling.astype(jnp.float32)
    corner_terms = jnp.einsum('gsacm,gsram->rgsac', coupling, blocks).reshape(LOADS, -1)
    flat_ids = corner_ids.reshape(-1)
    coarse_load = jnp.zeros((LOADS, COARSE), jnp.float32).at[:, flat_ids].add(corner_terms)
    coarse_values = jnp.dot(coarse_load.astype(jnp.bfloat16), coarse_inverse.T, preferred_element_type=jnp.float32)
    at_corners = coarse_values[:, flat_ids].astype(jnp.bfloat16).astype(jnp.float32)
    at_corners = at_corners.reshape(LOADS, N_GRP, N_SUB, SUBS_DEV, CORNERS)
    correction = jnp.einsum('gsacm,rgsac->gsram', coupling, at_corners).reshape(N_GRP, N_SUB, LOADS, SUBS_DEV * IFACE)
    return local_part + correction


def reference(loads, boundary_values, dirichlet_ids, dirichlet_coupling, local_inverse, local_schur, corner_coupling, corner_ids, coarse_inverse, row_counts, slot_of):
    inverse, live = slot_tables(row_counts, slot_of)
    live_field = live[:, :, None, :]

    def jumps(values):
        return live_field * (values - partner(values, slot_of, inverse))

    def dual(field):
        return jumps(apply_tilde(field.astype(jnp.bfloat16), local_inverse, corner_coupling, corner_ids, coarse_inverse))

    picked = boundary_values[:, dirichlet_ids].astype(jnp.bfloat16).astype(jnp.float32)
    lifted_part = jnp.einsum('gsand,rgsad->gsran', dirichlet_coupling.astype(jnp.float32), picked)
    lifted_part = lifted_part.reshape(N_GRP, N_SUB, LOADS, SUBS_DEV * IFACE)
    lifted = live_field * (loads.astype(jnp.float32) - lifted_part)
    jump_field = dual(lifted)
    multipliers = jnp.zeros_like(jump_field)
    residual = jump_field
    search = jump_field
    inner_before = jnp.ones((LOADS,), jnp.float32)
    for step in range(ITERS):
        smoothed = block_apply(local_schur, residual.astype(jnp.bfloat16))
        precond = 0.25 * live_field * (smoothed - partner(smoothed, slot_of, inverse))
        inner_now = jnp.sum(residual * precond, axis=(0, 1, 3))
        if step == 0:
            search = precond
        else:
            search = precond + (inner_now / inner_before)[None, None, :, None] * search
        image = dual(search)
        curvature = jnp.sum(search * image, axis=(0, 1, 3))
        step_size = (inner_now / curvature)[None, None, :, None]
        multipliers = multipliers + step_size * search
        residual = residual - step_size * image
        inner_before = inner_now
    return multipliers, residual
```

```python
import jax
import jax.numpy as jnp
from jax import lax
from jax.experimental import pallas as pl
from jax.experimental.pallas import tpu as pltpu
from jax.sharding import PartitionSpec as P
import functools

IFACE = 512
SUBS_DEV = 3
LOADS = 16
CORNERS = 24
SLAB_ROWS = 256
ITERS = 2
LANES = 128
WHOLE_COARSE_BYTES = 4 << 20


def extended(cells, sides, width):
    for axis, dim in sides:
        count = lax.axis_size(axis)
        ends = count - 1
        head = lax.slice_in_dim(cells, 0, width, axis=dim)
        tail = lax.slice_in_dim(cells, cells.shape[dim] - width, cells.shape[dim], axis=dim)
        cells = jnp.concatenate(
            [
                lax.ppermute(tail, axis, [(i, (i + 1) % count) for i in range(ends)]),
                cells,
                lax.ppermute(head, axis, [((i + 1) % count, i) for i in range(ends)]),
            ],
            axis=dim,
        )
    return cells


def spread_device(
    loads,
    boundary_values,
    dirichlet_ids,
    dirichlet_coupling,
    local_inverse,
    local_schur,
    corner_coupling,
    corner_ids,
    coarse_inverse,
    row_counts,
    slot_of,
):
    load_cases = loads[0, 0]
    fixed_ids = dirichlet_ids[0, 0]
    fixed_coupling = dirichlet_coupling[0, 0]
    inverse_blocks = local_inverse[0, 0]
    schur_blocks = local_schur[0, 0]
    coupling = corner_coupling[0, 0]
    corner_index = corner_ids[0, 0].reshape(-1)
    counts = row_counts[0, 0]
    slots = slot_of[0, 0]
    n_sub = lax.axis_size("sub")
    length = slots.shape[0]
    peer_rows = (length - 2 * SLAB_ROWS) // n_sub
    within = n_sub * peer_rows
    coarse_size = coarse_inverse.shape[1]
    positions = jnp.arange(length, dtype=jnp.int32)
    slot_inverse = jnp.zeros(length, jnp.int32).at[slots].set(positions)
    column = jnp.where(
        positions < within, positions // peer_rows, n_sub + (positions - within) // SLAB_ROWS
    )
    offset = jnp.where(positions < within, positions % peer_rows, (positions - within) % SLAB_ROWS)
    canon_live = (offset < counts[column]).astype(jnp.float32)
    live_mask = canon_live[slot_inverse][None, :]
    peer_index = slots[:within].reshape(n_sub, peer_rows)
    slab_index = slots[within:].reshape(2, SLAB_ROWS)
    slab_block = lax.all_to_all(coarse_inverse, "sub", split_axis=1, concat_axis=0, tiled=True)

    def partner(values):
        outgoing = jnp.take(values, peer_index, axis=1)
        incoming = lax.all_to_all(outgoing, "sub", split_axis=1, concat_axis=1, tiled=True).reshape(
            LOADS, within
        )
        slab_part = jnp.take(values, slab_index, axis=1)
        padded = extended(slab_part, (("grp", 1),), 1)
        joined = jnp.concatenate([incoming, padded[:, 0], padded[:, 3]], axis=1)
        return jnp.take(joined, slot_inverse, axis=1)

    def apply_tilde(field_b):
        blocks = field_b.reshape(LOADS, SUBS_DEV, IFACE)
        local_part = jnp.einsum(
            "anm,ram->ran", inverse_blocks, blocks, preferred_element_type=jnp.float32
        )
        corner_terms = jnp.einsum(
            "acm,ram->rac", coupling, blocks, preferred_element_type=jnp.float32
        )
        partial_load = (
            jnp.zeros((LOADS, coarse_size), jnp.float32)
            .at[:, corner_index]
            .add(corner_terms.reshape(LOADS, -1))
        )
        column_load = lax.psum_scatter(partial_load, "sub", scatter_dimension=1, tiled=True)
        column_total = lax.psum(column_load, "grp")
        block_term = jnp.einsum(
            "rj,ij->ri",
            column_total.astype(jnp.bfloat16),
            slab_block,
            preferred_element_type=jnp.float32,
        )
        slab_values = lax.psum(block_term, "sub")
        coarse_values = lax.all_gather(slab_values, "grp", axis=1, tiled=True)
        at_corners = (
            jnp.take(coarse_values, corner_index, axis=1)
            .astype(jnp.bfloat16)
            .reshape(LOADS, SUBS_DEV, CORNERS)
        )
        correction = jnp.einsum(
            "acm,rac->ram", coupling, at_corners, preferred_element_type=jnp.float32
        )
        return (local_part + correction).reshape(LOADS, length)

    def jumps(values):
        return live_mask * (values - partner(values))

    picked = jnp.take(boundary_values, fixed_ids, axis=1).astype(jnp.bfloat16)
    lifted_part = jnp.einsum(
        "and,rad->ran", fixed_coupling, picked, preferred_element_type=jnp.float32
    ).reshape(LOADS, length)
    lifted = live_mask * (load_cases.astype(jnp.float32) - lifted_part)
    jump_field = jumps(apply_tilde(lifted.astype(jnp.bfloat16)))
    multipliers = jnp.zeros_like(jump_field)
    residual = jump_field
    search = jump_field
    inner_before = jnp.ones((LOADS,), jnp.float32)
    for step in range(ITERS):
        smoothed = jnp.einsum(
            "anm,ram->ran",
            schur_blocks,
            residual.astype(jnp.bfloat16).reshape(LOADS, SUBS_DEV, IFACE),
            preferred_element_type=jnp.float32,
        ).reshape(LOADS, length)
        precond = 0.25 * live_mask * (smoothed - partner(smoothed))
        inner_now = lax.psum(jnp.sum(residual * precond, axis=1), ("grp", "sub"))
        if step == 0:
            search = precond
        else:
            search = precond + (inner_now / inner_before)[:, None] * search
        tilde = apply_tilde(search.astype(jnp.bfloat16))
        image = jumps(tilde)
        curvature = lax.psum(jnp.sum(search * image, axis=1), ("grp", "sub"))
        step_size = (inner_now / curvature)[:, None]
        multipliers = multipliers + step_size * search
        residual = residual - step_size * image
        inner_before = inner_now
    return (multipliers[None, None], residual[None, None])


F32 = jnp.float32
BF16 = jnp.bfloat16
MESH = pl.DeviceIdType.MESH
NT = (((1,), (1,)), ((), ()))


def mm(a, b):
    return jnp.dot(a, b, preferred_element_type=F32)


def mm_nt(a, b):
    return lax.dot_general(a, b, NT, preferred_element_type=F32)


def onehot(ids_row, first, rows):
    place = lax.broadcasted_iota(jnp.int32, (rows, ids_row.shape[1]), 0) + first
    return jnp.where(place == ids_row, 1.0, 0.0).astype(BF16)


def fused_kernel(
    n_grp, n_sub, peer_rows, coarse,
    loads_ref, bound_ref, fixed_ref, fixcpl_ref, inv_ref, schur_ref, cpl_ref, target_ref, cinv_ref,
    counts_ref, slots_ref,
    mult_ref, res_ref,
    perm, cplf, cplb, cinvf, cinvb, place, ids_all, cinv_all, to_peer, from_peer, to_slab, from_slab,
    slab_terms, slab_loads,
    id_send, id_recv, cz_send, cz_recv, cg_send, cg_recv,
    p_send, p_recv, h_send, h_recv, t_send, t_recv, l_send, l_recv,
):
    g = lax.axis_index("grp")
    s = lax.axis_index("sub")
    length = slots_ref.shape[1]
    within = n_sub * peer_rows
    corners = SUBS_DEV * CORNERS
    own_rows = coarse // (n_grp * n_sub)

    ids_all[s] = target_ref[...]
    cinv_all[g, s] = cinv_ref[...]
    from_peer[...] = jnp.zeros_like(from_peer)
    from_slab[...] = jnp.zeros_like(from_slab)

    barrier = pltpu.get_barrier_semaphore()
    for k in range(1, n_sub):
        pl.semaphore_signal(barrier, inc=1, device_id=(g, lax.rem(s + k, n_sub)), device_id_type=MESH)
    for k in range(1, n_grp):
        pl.semaphore_signal(barrier, inc=1, device_id=(lax.rem(g + k, n_grp), s), device_id_type=MESH)
    pl.semaphore_wait(barrier, n_sub + n_grp - 2)

    def over_sub(buf_at, send, recv):
        copies = []
        for k in range(1, n_sub):
            copies.append(pltpu.make_async_remote_copy(
                src_ref=buf_at, dst_ref=buf_at, send_sem=send.at[k], recv_sem=recv.at[k],
                device_id=(g, lax.rem(s + k, n_sub)), device_id_type=MESH))
        for copy in copies:
            copy.start()
        return copies

    def over_grp(buf_at, send, recv):
        copies = []
        for k in range(1, n_grp):
            copies.append(pltpu.make_async_remote_copy(
                src_ref=buf_at, dst_ref=buf_at, send_sem=send.at[k], recv_sem=recv.at[k],
                device_id=(lax.rem(g + k, n_grp), s), device_id_type=MESH))
        for copy in copies:
            copy.start()
        return copies

    id_copies = over_sub(ids_all.at[s], id_send, id_recv)
    cz_copies = over_sub(cinv_all.at[g, s], cz_send, cz_recv)

    chunk = 128

    @pl.loop(0, length // chunk)
    def _(i):
        start = pl.multiple_of(i * chunk, chunk)
        perm[pl.ds(start, chunk), :] = onehot(slots_ref[...], start, chunk)

    column = lax.broadcasted_iota(jnp.int32, (LOADS, length), 1)
    low = jnp.zeros((LOADS, length), jnp.int32)
    count = jnp.zeros((LOADS, length), jnp.int32)
    for p in range(n_sub + 2):
        first = p * peer_rows if p <= n_sub else within + SLAB_ROWS
        low = jnp.where(column >= first, first, low)
        count = jnp.where(column >= first, counts_ref[p], count)
    canon_live = jnp.where(column - low < count, 1.0, 0.0).astype(BF16)
    live = mm_nt(canon_live, perm[...])

    cplf[...] = jnp.zeros_like(cplf)
    for a in range(SUBS_DEV):
        cplf[a * CORNERS:(a + 1) * CORNERS, a * IFACE:(a + 1) * IFACE] = cpl_ref[a].astype(F32)
    cplb[...] = cplf[...].astype(BF16)

    bound = bound_ref[...].astype(BF16)
    lifts = []
    for a in range(SUBS_DEV):
        picked = mm(bound, onehot(fixed_ref[a:a + 1, :], 0, bound_ref.shape[1]))
        lifts.append(mm_nt(picked.astype(BF16), fixcpl_ref[a]))
    lifted = live * (loads_ref[...].astype(F32) - jnp.concatenate(lifts, axis=1))

    for copy in cz_copies:
        copy.wait()
    cg_copies = over_grp(cinv_all.at[g], cg_send, cg_recv)
    for copy in id_copies:
        copy.wait()
    for q in range(n_sub):
        place[:, q * LANES:(q + 1) * LANES] = onehot(ids_all[q], 0, coarse + LANES)
    own_place = onehot(target_ref[...], 0, coarse)

    def blocks_apply(ref, field_b):
        return jnp.concatenate(
            [mm(field_b[:, a * IFACE:(a + 1) * IFACE], ref[a]) for a in range(SUBS_DEV)], axis=1)

    lane = lax.broadcasted_iota(jnp.int32, (LOADS, LANES), 1)

    def row_sum(x):
        return jnp.sum(x, axis=1, keepdims=True)

    def tilde(i, field, extra):
        field_b = field.astype(BF16)
        message = mm_nt(field_b, cplb[...])
        local = blocks_apply(inv_ref, field_b)
        sums = extra(local)
        for k, part in enumerate(sums):
            message = jnp.where(lane == corners + k, part, message)
        slab_terms[i, s] = message
        for copy in over_sub(slab_terms.at[i, s], t_send.at[i], t_recv.at[i]):
            copy.wait()
        terms = jnp.concatenate([slab_terms[i, q] for q in range(n_sub)], axis=1)
        high = terms.astype(BF16)
        rest = (terms - high.astype(F32)).astype(BF16)
        both = mm_nt(jnp.concatenate([high, rest], axis=0), place[...])
        dense = both[:LOADS] + both[LOADS:]
        total = dense[:, coarse:]
        total_high = total.astype(BF16)
        slab_loads[i, g] = jnp.concatenate(
            [dense[:, :coarse].astype(BF16), total_high, (total - total_high.astype(F32)).astype(BF16)], axis=1)
        for copy in over_grp(slab_loads.at[i, g], l_send.at[i], l_recv.at[i]):
            copy.wait()
        if i == 0:
            for copy in cg_copies:
                copy.wait()
            for d in range(n_grp * n_sub):
                part = cinv_all[d // n_sub, d % n_sub].astype(F32)
                cinvf[d * own_rows:(d + 1) * own_rows, :] = part[:own_rows]
            cinvb[...] = cinvf[...].astype(BF16)
        whole = slab_loads[i, 0].astype(F32)
        for q in range(1, n_grp):
            whole = whole + slab_loads[i, q].astype(F32)
        load = whole[:, :coarse]
        values = mm(load.astype(BF16), cinvb[...])
        corner_values = mm(values.astype(BF16), own_place)
        result = local + mm(corner_values.astype(BF16), cplb[...])
        scalars = whole[:, coarse:coarse + LANES] + whole[:, coarse + LANES:]
        found = [row_sum(jnp.where(lane == k, scalars, 0.0)) for k in range(len(sums))]
        return result, local, load, values, found

    def partner(i, field):
        out = mm(field.astype(BF16), perm[...]).astype(BF16)
        for q in range(n_sub):
            to_peer[i, q] = out[:, q * peer_rows:(q + 1) * peer_rows]
        for q in range(2):
            to_slab[i, q] = out[:, within + q * SLAB_ROWS:within + (q + 1) * SLAB_ROWS]
        down = pltpu.make_async_remote_copy(
            src_ref=to_slab.at[i, 0], dst_ref=from_slab.at[i, 1], send_sem=h_send.at[i, 0],
            recv_sem=h_recv.at[i, 1], device_id=(jnp.maximum(g - 1, 0), s), device_id_type=MESH)
        up = pltpu.make_async_remote_copy(
            src_ref=to_slab.at[i, 1], dst_ref=from_slab.at[i, 0], send_sem=h_send.at[i, 1],
            recv_sem=h_recv.at[i, 0], device_id=(jnp.minimum(g + 1, n_grp - 1), s), device_id_type=MESH)

        @pl.when(g > 0)
        def _():
            down.start()

        @pl.when(g < n_grp - 1)
        def _():
            up.start()

        copies = []
        for k in range(1, n_sub):
            to = lax.rem(s + k, n_sub)
            copies.append(pltpu.make_async_remote_copy(
                src_ref=to_peer.at[i, to], dst_ref=from_peer.at[i, s], send_sem=p_send.at[i, k],
                recv_sem=p_recv.at[i, k], device_id=(g, to), device_id_type=MESH))
        for copy in copies:
            copy.start()
        for copy in copies:
            copy.wait()

        @pl.when(g > 0)
        def _():
            down.wait_send()
            up.wait_recv()

        @pl.when(g < n_grp - 1)
        def _():
            up.wait_send()
            down.wait_recv()

        joined = jnp.concatenate(
            [from_peer[i, q] for q in range(n_sub)] + [from_slab[i, q] for q in range(2)], axis=1)
        return mm_nt(joined, perm[...])

    def smoothed(residual):
        return blocks_apply(schur_ref, residual.astype(BF16))

    image = tilde(0, lifted, lambda local: [])[0]
    residual = live * (image - partner(0, image))

    smooth = smoothed(residual)
    inner_part = 0.5 * row_sum(residual * smooth)
    first = 0.25 * live * (smooth - partner(1, smooth))
    image0, local0, load0, values0, (inner0, energy0) = tilde(
        1, first, lambda local: [inner_part, row_sum(first * local)])
    energy0 = energy0 + row_sum(load0 * values0)
    size0 = inner0 / (2.0 * energy0)
    residual = residual - size0 * (live * (image0 - partner(2, image0)))

    smooth = smoothed(residual)
    inner_part1 = 0.5 * row_sum(residual * smooth)
    second = 0.25 * live * (smooth - partner(3, smooth))
    image1, _, load1, values1, (inner1, energy1, cross) = tilde(
        2, second, lambda local: [inner_part1, row_sum(second * local), row_sum(second * local0)])
    ratio = inner1 / inner0
    energy1 = energy1 + row_sum(load1 * values1)
    cross = cross + row_sum(load1 * values0)
    energy = energy1 + ratio * (2.0 * cross + ratio * energy0)
    size1 = inner1 / (2.0 * energy)
    search = second + ratio * first
    image = image1 + ratio * image0
    mult_ref[...] = size0 * first + size1 * search
    res_ref[...] = residual - size1 * (live * (image - partner(4, image)))


def fused_device(
    loads,
    boundary_values,
    dirichlet_ids,
    dirichlet_coupling,
    local_inverse,
    local_schur,
    corner_coupling,
    corner_ids,
    coarse_inverse,
    row_counts,
    slot_of,
):
    n_grp, n_sub = lax.axis_size("grp"), lax.axis_size("sub")
    length = slot_of.shape[2]
    peer_rows = (length - 2 * SLAB_ROWS) // n_sub
    coarse = coarse_inverse.shape[1]
    corners = SUBS_DEV * CORNERS
    target = jnp.concatenate(
        [corner_ids[0, 0].reshape(1, corners), coarse + jnp.arange(LANES - corners, dtype=jnp.int32)[None]], axis=1)
    rows = coarse_inverse.shape[0]
    held = -(-rows // 16) * 16
    coarse_rows = jnp.pad(coarse_inverse, ((0, held - rows), (0, 0)))
    vmem = pl.BlockSpec(memory_space=pltpu.VMEM)
    smem = pl.BlockSpec(memory_space=pltpu.SMEM)
    swaps, solves = 2 * ITERS + 1, ITERS + 1
    dma = pltpu.SemaphoreType.DMA
    field = jax.ShapeDtypeStruct((LOADS, length), F32)
    mult, res = pl.pallas_call(
        functools.partial(fused_kernel, n_grp, n_sub, peer_rows, coarse),
        out_shape=(field, field),
        in_specs=[vmem] * 9 + [smem, vmem],
        out_specs=(vmem, vmem),
        scratch_shapes=[
            pltpu.VMEM((length, length), BF16),
            pltpu.VMEM((LANES, length), F32),
            pltpu.VMEM((LANES, length), BF16),
            pltpu.VMEM((coarse, coarse), F32),
            pltpu.VMEM((coarse, coarse), BF16),
            pltpu.VMEM((coarse + LANES, n_sub * LANES), BF16),
            pltpu.VMEM((n_sub, 1, LANES), jnp.int32),
            pltpu.VMEM((n_grp, n_sub, held, coarse), BF16),
            pltpu.VMEM((swaps, n_sub, LOADS, peer_rows), BF16),
            pltpu.VMEM((swaps, n_sub, LOADS, peer_rows), BF16),
            pltpu.VMEM((swaps, 2, LOADS, SLAB_ROWS), BF16),
            pltpu.VMEM((swaps, 2, LOADS, SLAB_ROWS), BF16),
            pltpu.VMEM((solves, n_sub, LOADS, LANES), F32),
            pltpu.VMEM((solves, n_grp, LOADS, coarse + 2 * LANES), BF16),
            dma((n_sub,)), dma((n_sub,)), dma((n_sub,)), dma((n_sub,)), dma((n_grp,)), dma((n_grp,)),
            dma((swaps, n_sub)), dma((swaps, n_sub)), dma((swaps, 2)), dma((swaps, 2)),
            dma((solves, n_sub)), dma((solves, n_sub)), dma((solves, n_grp)), dma((solves, n_grp)),
        ],
        compiler_params=pltpu.CompilerParams(
            collective_id=0, has_side_effects=True, vmem_limit_bytes=48 << 20),
    )(
        loads[0, 0], boundary_values, dirichlet_ids[0, 0], dirichlet_coupling[0, 0], local_inverse[0, 0],
        local_schur[0, 0], corner_coupling[0, 0], target, coarse_rows, row_counts[0, 0], slot_of[0],
    )
    return (mult[None, None], res[None, None])


def per_device(*args):
    coarse = args[8].shape[1]
    peer_rows = (args[10].shape[2] - 2 * SLAB_ROWS) // lax.axis_size("sub")
    small = coarse * coarse * args[8].dtype.itemsize <= WHOLE_COARSE_BYTES
    aligned = peer_rows % LANES == 0 and coarse % LANES == 0 and args[8].shape[0] % 8 == 0
    return (fused_device if small and aligned else spread_device)(*args)


def solution(mesh):
    in_specs = (
        P("grp", "sub", None, None),
        P(),
        P("grp", "sub", None, None),
        P("grp", "sub", None, None, None),
        P("grp", "sub", None, None, None),
        P("grp", "sub", None, None, None),
        P("grp", "sub", None, None, None),
        P("grp", "sub", None, None),
        P(("grp", "sub"), None),
        P("grp", "sub", None),
        P("grp", "sub", None),
    )
    out_specs = (P("grp", "sub", None, None), P("grp", "sub", None, None))
    return jax.shard_map(
        per_device, mesh=mesh, in_specs=in_specs, out_specs=out_specs, check_vma=False
    )
```

```python
import jax
import jax.numpy as jnp
from jax import lax
from jax.experimental import pallas as pl
from jax.experimental.pallas import tpu as pltpu
from jax.sharding import PartitionSpec as P
import functools

IFACE = 512
SUBS_DEV = 3
LOADS = 16
CORNERS = 24
SLAB_ROWS = 256
ITERS = 2
LANES = 128
WHOLE_COARSE_BYTES = 4 << 20


def extended(cells, sides, width):
    for axis, dim in sides:
        count = lax.axis_size(axis)
        ends = count - 1
        head = lax.slice_in_dim(cells, 0, width, axis=dim)
        tail = lax.slice_in_dim(cells, cells.shape[dim] - width, cells.shape[dim], axis=dim)
        cells = jnp.concatenate(
            [
                lax.ppermute(tail, axis, [(i, (i + 1) % count) for i in range(ends)]),
                cells,
                lax.ppermute(head, axis, [((i + 1) % count, i) for i in range(ends)]),
            ],
            axis=dim,
        )
    return cells


def spread_device(
    loads,
    boundary_values,
    dirichlet_ids,
    dirichlet_coupling,
    local_inverse,
    local_schur,
    corner_coupling,
    corner_ids,
    coarse_inverse,
    row_counts,
    slot_of,
):
    load_cases = loads[0, 0]
    fixed_ids = dirichlet_ids[0, 0]
    fixed_coupling = dirichlet_coupling[0, 0]
    inverse_blocks = local_inverse[0, 0]
    schur_blocks = local_schur[0, 0]
    coupling = corner_coupling[0, 0]
    corner_index = corner_ids[0, 0].reshape(-1)
    counts = row_counts[0, 0]
    slots = slot_of[0, 0]
    n_sub = lax.axis_size("sub")
    length = slots.shape[0]
    peer_rows = (length - 2 * SLAB_ROWS) // n_sub
    within = n_sub * peer_rows
    coarse_size = coarse_inverse.shape[1]
    positions = jnp.arange(length, dtype=jnp.int32)
    slot_inverse = jnp.zeros(length, jnp.int32).at[slots].set(positions)
    column = jnp.where(
        positions < within, positions // peer_rows, n_sub + (positions - within) // SLAB_ROWS
    )
    offset = jnp.where(positions < within, positions % peer_rows, (positions - within) % SLAB_ROWS)
    canon_live = (offset < counts[column]).astype(jnp.float32)
    live_mask = canon_live[slot_inverse][None, :]
    peer_index = slots[:within].reshape(n_sub, peer_rows)
    slab_index = slots[within:].reshape(2, SLAB_ROWS)
    slab_block = lax.all_to_all(coarse_inverse, "sub", split_axis=1, concat_axis=0, tiled=True)

    def partner(values):
        outgoing = jnp.take(values, peer_index, axis=1)
        incoming = lax.all_to_all(outgoing, "sub", split_axis=1, concat_axis=1, tiled=True).reshape(
            LOADS, within
        )
        slab_part = jnp.take(values, slab_index, axis=1)
        padded = extended(slab_part, (("grp", 1),), 1)
        joined = jnp.concatenate([incoming, padded[:, 0], padded[:, 3]], axis=1)
        return jnp.take(joined, slot_inverse, axis=1)

    def apply_tilde(field_b):
        blocks = field_b.reshape(LOADS, SUBS_DEV, IFACE)
        local_part = jnp.einsum(
            "anm,ram->ran", inverse_blocks, blocks, preferred_element_type=jnp.float32
        )
        corner_terms = jnp.einsum(
            "acm,ram->rac", coupling, blocks, preferred_element_type=jnp.float32
        )
        partial_load = (
            jnp.zeros((LOADS, coarse_size), jnp.float32)
            .at[:, corner_index]
            .add(corner_terms.reshape(LOADS, -1))
        )
        column_load = lax.psum_scatter(partial_load, "sub", scatter_dimension=1, tiled=True)
        column_total = lax.psum(column_load, "grp")
        block_term = jnp.einsum(
            "rj,ij->ri",
            column_total.astype(jnp.bfloat16),
            slab_block,
            preferred_element_type=jnp.float32,
        )
        slab_values = lax.psum(block_term, "sub")
        coarse_values = lax.all_gather(slab_values, "grp", axis=1, tiled=True)
        at_corners = (
            jnp.take(coarse_values, corner_index, axis=1)
            .astype(jnp.bfloat16)
            .reshape(LOADS, SUBS_DEV, CORNERS)
        )
        correction = jnp.einsum(
            "acm,rac->ram", coupling, at_corners, preferred_element_type=jnp.float32
        )
        return (local_part + correction).reshape(LOADS, length)

    def jumps(values):
        return live_mask * (values - partner(values))

    picked = jnp.take(boundary_values, fixed_ids, axis=1).astype(jnp.bfloat16)
    lifted_part = jnp.einsum(
        "and,rad->ran", fixed_coupling, picked, preferred_element_type=jnp.float32
    ).reshape(LOADS, length)
    lifted = live_mask * (load_cases.astype(jnp.float32) - lifted_part)
    jump_field = jumps(apply_tilde(lifted.astype(jnp.bfloat16)))
    multipliers = jnp.zeros_like(jump_field)
    residual = jump_field
    search = jump_field
    inner_before = jnp.ones((LOADS,), jnp.float32)
    for step in range(ITERS):
        smoothed = jnp.einsum(
            "anm,ram->ran",
            schur_blocks,
            residual.astype(jnp.bfloat16).reshape(LOADS, SUBS_DEV, IFACE),
            preferred_element_type=jnp.float32,
        ).reshape(LOADS, length)
        precond = 0.25 * live_mask * (smoothed - partner(smoothed))
        inner_now = lax.psum(jnp.sum(residual * precond, axis=1), ("grp", "sub"))
        if step == 0:
            search = precond
        else:
            search = precond + (inner_now / inner_before)[:, None] * search
        tilde = apply_tilde(search.astype(jnp.bfloat16))
        image = jumps(tilde)
        curvature = lax.psum(jnp.sum(search * image, axis=1), ("grp", "sub"))
        step_size = (inner_now / curvature)[:, None]
        multipliers = multipliers + step_size * search
        residual = residual - step_size * image
        inner_before = inner_now
    return (multipliers[None, None], residual[None, None])


F32 = jnp.float32
BF16 = jnp.bfloat16
MESH = pl.DeviceIdType.MESH
NT = (((1,), (1,)), ((), ()))


def mm(a, b):
    return jnp.dot(a, b, preferred_element_type=F32)


def mm_nt(a, b):
    return lax.dot_general(a, b, NT, preferred_element_type=F32)


def onehot(ids_row, first, rows):
    place = lax.broadcasted_iota(jnp.int32, (rows, ids_row.shape[1]), 0) + first
    return jnp.where(place == ids_row, 1.0, 0.0).astype(BF16)


def fused_kernel(
    n_grp, n_sub, peer_rows, coarse,
    loads_hbm, bound_hbm, fixcpl_hbm, inv_hbm, schur_hbm, cpl_hbm, slots_hbm, fixed_ref, target_ref, cinv_ref,
    counts_ref,
    mult_ref, res_ref,
    loads_ref, bound_ref, fixcpl_ref, inv_ref, schur_ref, cpl_ref, slots_ref, fetched,
    perm, perm_t, cplf, cplb, cinvf, cinvb, place, ids_all, cinv_all, to_peer, from_peer, to_slab, from_slab,
    slab_terms, slab_loads,
    id_send, id_recv, cz_send, cz_recv, cg_send, cg_recv,
    p_send, p_recv, h_send, h_recv, t_send, t_recv, l_send, l_recv,
):
    g = lax.axis_index("grp")
    s = lax.axis_index("sub")
    length = slots_ref.shape[1]
    fetch = {}
    for k, (name, source, held) in enumerate([
        ("bound", bound_hbm, bound_ref), ("fixcpl", fixcpl_hbm, fixcpl_ref), ("slots", slots_hbm, slots_ref),
        ("loads", loads_hbm, loads_ref), ("cpl", cpl_hbm, cpl_ref), ("inv", inv_hbm, inv_ref),
        ("schur", schur_hbm, schur_ref),
    ]):
        fetch[name] = pltpu.make_async_copy(source, held, fetched.at[k])
        fetch[name].start()
    within = n_sub * peer_rows
    corners = SUBS_DEV * CORNERS
    own_rows = coarse // (n_grp * n_sub)

    ids_all[s] = target_ref[...]
    cinv_all[g, s] = cinv_ref[...]
    from_peer[...] = jnp.zeros_like(from_peer)
    from_slab[...] = jnp.zeros_like(from_slab)

    barrier = pltpu.get_barrier_semaphore()
    for k in range(1, n_sub):
        pl.semaphore_signal(barrier, inc=1, device_id=(g, lax.rem(s + k, n_sub)), device_id_type=MESH)
    for k in range(1, n_grp):
        pl.semaphore_signal(barrier, inc=1, device_id=(lax.rem(g + k, n_grp), s), device_id_type=MESH)
    pl.semaphore_wait(barrier, n_sub + n_grp - 2)

    def over_sub(buf_at, send, recv):
        copies = []
        for k in range(1, n_sub):
            copies.append(pltpu.make_async_remote_copy(
                src_ref=buf_at, dst_ref=buf_at, send_sem=send.at[k], recv_sem=recv.at[k],
                device_id=(g, lax.rem(s + k, n_sub)), device_id_type=MESH))
        for copy in copies:
            copy.start()
        return copies

    def over_grp(buf_at, send, recv):
        copies = []
        for k in range(1, n_grp):
            copies.append(pltpu.make_async_remote_copy(
                src_ref=buf_at, dst_ref=buf_at, send_sem=send.at[k], recv_sem=recv.at[k],
                device_id=(lax.rem(g + k, n_grp), s), device_id_type=MESH))
        for copy in copies:
            copy.start()
        return copies

    mate = g + 1 - 2 * lax.rem(g, 2)

    def coarse_rows_to(k, device, block):
        return pltpu.make_async_remote_copy(
            src_ref=cinv_all.at[block], dst_ref=cinv_all.at[block], send_sem=cg_send.at[k], recv_sem=cg_recv.at[k],
            device_id=(device, s), device_id_type=MESH)

    cz_copies = over_sub(cinv_all.at[g, s], cz_send, cz_recv)
    id_copies = over_sub(ids_all.at[s], id_send, id_recv)

    fetch["bound"].wait()
    fetch["fixcpl"].wait()
    bound = bound_ref[...].astype(BF16)
    lifts = []
    for a in range(SUBS_DEV):
        picked = mm(bound, onehot(fixed_ref[a:a + 1, :], 0, bound_ref.shape[1]))
        lifts.append(mm_nt(picked.astype(BF16), fixcpl_ref[a]))
    lift = jnp.concatenate(lifts, axis=1)

    for copy in cz_copies:
        copy.wait()
    cg_direct = [coarse_rows_to(k, lax.rem(g + k, n_grp), g) for k in range(2, n_grp, 2)]
    cg_passed = [coarse_rows_to(k + 1, mate, lax.rem(g + n_grp - k, n_grp)) for k in range(0, n_grp, 2)]
    for copy in cg_direct + cg_passed[:1]:
        copy.start()

    chunk = LANES
    fetch["slots"].wait()

    @pl.loop(0, length // chunk)
    def _(i):
        start = pl.multiple_of(i * chunk, chunk)
        perm[pl.ds(start, chunk), :] = onehot(slots_ref[...], start, chunk)
        ids = jnp.broadcast_to(slots_ref[:, pl.ds(start, chunk)].astype(F32), (chunk, chunk))
        ids = jnp.transpose(ids).astype(jnp.int32)
        for c in range(length // LANES):
            at = lax.broadcasted_iota(jnp.int32, (chunk, LANES), 1) + c * LANES
            perm_t[pl.ds(start, chunk), c * LANES:(c + 1) * LANES] = jnp.where(at == ids, 1.0, 0.0).astype(BF16)

    column = lax.broadcasted_iota(jnp.int32, (LOADS, length), 1)
    low = jnp.zeros((LOADS, length), jnp.int32)
    count = jnp.zeros((LOADS, length), jnp.int32)
    for p in range(n_sub + 2):
        first = p * peer_rows if p <= n_sub else within + SLAB_ROWS
        low = jnp.where(column >= first, first, low)
        count = jnp.where(column >= first, counts_ref[p], count)
    canon_live = jnp.where(column - low < count, 1.0, 0.0).astype(BF16)
    live = mm(canon_live, perm_t[...])

    fetch["cpl"].wait()
    cplf[...] = jnp.zeros_like(cplf)
    for a in range(SUBS_DEV):
        cplf[a * CORNERS:(a + 1) * CORNERS, a * IFACE:(a + 1) * IFACE] = cpl_ref[a].astype(F32)
    cplb[...] = cplf[...].astype(BF16)

    fetch["loads"].wait()
    lifted = live * (loads_ref[...].astype(F32) - lift)

    for copy in id_copies:
        copy.wait()
    for q in range(n_sub):
        place[:, q * LANES:(q + 1) * LANES] = onehot(ids_all[q], 0, coarse + LANES)
    own_place = onehot(target_ref[...], 0, coarse)

    fetch["inv"].wait()
    fetch["schur"].wait()

    def blocks_apply(ref, field_b):
        return jnp.concatenate(
            [mm(field_b[:, a * IFACE:(a + 1) * IFACE], ref[a]) for a in range(SUBS_DEV)], axis=1)

    lane = lax.broadcasted_iota(jnp.int32, (LOADS, LANES), 1)

    def row_sum(x):
        return jnp.sum(x, axis=1, keepdims=True)

    def tilde(i, field, extra):
        field_b = field.astype(BF16)
        message = mm_nt(field_b, cplb[...])
        local = blocks_apply(inv_ref, field_b)
        sums = extra(local)
        for k, part in enumerate(sums):
            message = jnp.where(lane == corners + k, part, message)
        slab_terms[i, s] = message
        for copy in over_sub(slab_terms.at[i, s], t_send.at[i], t_recv.at[i]):
            copy.wait()
        terms = jnp.concatenate([slab_terms[i, q] for q in range(n_sub)], axis=1)
        high = terms.astype(BF16)
        rest = (terms - high.astype(F32)).astype(BF16)
        both = mm_nt(jnp.concatenate([high, rest], axis=0), place[...])
        dense = both[:LOADS] + both[LOADS:]
        total = dense[:, coarse:]
        total_high = total.astype(BF16)
        slab_loads[i, g] = jnp.concatenate(
            [dense[:, :coarse].astype(BF16), total_high, (total - total_high.astype(F32)).astype(BF16)], axis=1)
        load_copies = over_grp(slab_loads.at[i, g], l_send.at[i], l_recv.at[i])
        if i == 0:
            for copy, passed in zip(cg_direct, cg_passed[1:]):
                copy.wait()
                passed.start()
        for copy in load_copies:
            copy.wait()
        if i == 0:
            for copy in cg_passed:
                copy.wait()
            for d in range(n_grp * n_sub):
                part = cinv_all[d // n_sub, d % n_sub].astype(F32)
                cinvf[d * own_rows:(d + 1) * own_rows, :] = part[:own_rows]
            cinvb[...] = cinvf[...].astype(BF16)
        whole = slab_loads[i, 0].astype(F32)
        for q in range(1, n_grp):
            whole = whole + slab_loads[i, q].astype(F32)
        load = whole[:, :coarse]
        values = mm(load.astype(BF16), cinvb[...])
        corner_values = mm(values.astype(BF16), own_place)
        result = local + mm(corner_values.astype(BF16), cplb[...])
        scalars = whole[:, coarse:coarse + LANES] + whole[:, coarse + LANES:]
        found = [row_sum(jnp.where(lane == k, scalars, 0.0)) for k in range(len(sums))]
        return result, local, load, values, found

    def partner(i, field):
        out = mm(field.astype(BF16), perm[...]).astype(BF16)
        for q in range(n_sub):
            to_peer[i, q] = out[:, q * peer_rows:(q + 1) * peer_rows]
        for q in range(2):
            to_slab[i, q] = out[:, within + q * SLAB_ROWS:within + (q + 1) * SLAB_ROWS]
        down = pltpu.make_async_remote_copy(
            src_ref=to_slab.at[i, 0], dst_ref=from_slab.at[i, 1], send_sem=h_send.at[i, 0],
            recv_sem=h_recv.at[i, 1], device_id=(jnp.maximum(g - 1, 0), s), device_id_type=MESH)
        up = pltpu.make_async_remote_copy(
            src_ref=to_slab.at[i, 1], dst_ref=from_slab.at[i, 0], send_sem=h_send.at[i, 1],
            recv_sem=h_recv.at[i, 0], device_id=(jnp.minimum(g + 1, n_grp - 1), s), device_id_type=MESH)

        @pl.when(g > 0)
        def _():
            down.start()

        @pl.when(g < n_grp - 1)
        def _():
            up.start()

        copies = []
        for k in range(1, n_sub):
            to = lax.rem(s + k, n_sub)
            copies.append(pltpu.make_async_remote_copy(
                src_ref=to_peer.at[i, to], dst_ref=from_peer.at[i, s], send_sem=p_send.at[i, k],
                recv_sem=p_recv.at[i, k], device_id=(g, to), device_id_type=MESH))
        for copy in copies:
            copy.start()
        for copy in copies:
            copy.wait()

        @pl.when(g > 0)
        def _():
            down.wait_send()
            up.wait_recv()

        @pl.when(g < n_grp - 1)
        def _():
            up.wait_send()
            down.wait_recv()

        joined = jnp.concatenate(
            [from_peer[i, q] for q in range(n_sub)] + [from_slab[i, q] for q in range(2)], axis=1)
        return mm(joined, perm_t[...])

    def smoothed(residual):
        return blocks_apply(schur_ref, residual.astype(BF16))

    image = tilde(0, lifted, lambda local: [])[0]
    residual = live * (image - partner(0, image))

    smooth = smoothed(residual)
    inner_part = 0.5 * row_sum(residual * smooth)
    first = 0.25 * live * (smooth - partner(1, smooth))
    image0, local0, load0, values0, (inner0, energy0) = tilde(
        1, first, lambda local: [inner_part, row_sum(first * local)])
    energy0 = energy0 + row_sum(load0 * values0)
    size0 = inner0 / (2.0 * energy0)
    residual = residual - size0 * (live * (image0 - partner(2, image0)))

    smooth = smoothed(residual)
    inner_part1 = 0.5 * row_sum(residual * smooth)
    second = 0.25 * live * (smooth - partner(3, smooth))
    image1, _, load1, values1, (inner1, energy1, cross) = tilde(
        2, second, lambda local: [inner_part1, row_sum(second * local), row_sum(second * local0)])
    ratio = inner1 / inner0
    energy1 = energy1 + row_sum(load1 * values1)
    cross = cross + row_sum(load1 * values0)
    energy = energy1 + ratio * (2.0 * cross + ratio * energy0)
    size1 = inner1 / (2.0 * energy)
    search = second + ratio * first
    image = image1 + ratio * image0
    mult_ref[...] = size0 * first + size1 * search
    res_ref[...] = residual - size1 * (live * (image - partner(4, image)))


def fused_device(
    loads,
    boundary_values,
    dirichlet_ids,
    dirichlet_coupling,
    local_inverse,
    local_schur,
    corner_coupling,
    corner_ids,
    coarse_inverse,
    row_counts,
    slot_of,
):
    n_grp, n_sub = lax.axis_size("grp"), lax.axis_size("sub")
    length = slot_of.shape[2]
    peer_rows = (length - 2 * SLAB_ROWS) // n_sub
    coarse = coarse_inverse.shape[1]
    corners = SUBS_DEV * CORNERS
    target = jnp.concatenate(
        [corner_ids[0, 0].reshape(1, corners), coarse + jnp.arange(LANES - corners, dtype=jnp.int32)[None]], axis=1)
    rows = coarse_inverse.shape[0]
    held = -(-rows // 16) * 16
    coarse_rows = jnp.pad(coarse_inverse, ((0, held - rows), (0, 0)))
    vmem = pl.BlockSpec(memory_space=pltpu.VMEM)
    hbm = pl.BlockSpec(memory_space=pltpu.HBM)
    smem = pl.BlockSpec(memory_space=pltpu.SMEM)
    swaps, solves = 2 * ITERS + 1, ITERS + 1
    dma = pltpu.SemaphoreType.DMA
    field = jax.ShapeDtypeStruct((LOADS, length), F32)
    fetched = (
        loads[0, 0], boundary_values, dirichlet_coupling[0, 0], local_inverse[0, 0], local_schur[0, 0],
        corner_coupling[0, 0], slot_of[0],
    )
    mult, res = pl.pallas_call(
        functools.partial(fused_kernel, n_grp, n_sub, peer_rows, coarse),
        out_shape=(field, field),
        in_specs=[hbm] * 7 + [vmem] * 3 + [smem],
        out_specs=(vmem, vmem),
        scratch_shapes=[pltpu.VMEM(x.shape, x.dtype) for x in fetched] + [
            dma((len(fetched),)),
            pltpu.VMEM((length, length), BF16),
            pltpu.VMEM((length, length), BF16),
            pltpu.VMEM((LANES, length), F32),
            pltpu.VMEM((LANES, length), BF16),
            pltpu.VMEM((coarse, coarse), F32),
            pltpu.VMEM((coarse, coarse), BF16),
            pltpu.VMEM((coarse + LANES, n_sub * LANES), BF16),
            pltpu.VMEM((n_sub, 1, LANES), jnp.int32),
            pltpu.VMEM((n_grp, n_sub, held, coarse), BF16),
            pltpu.VMEM((swaps, n_sub, LOADS, peer_rows), BF16),
            pltpu.VMEM((swaps, n_sub, LOADS, peer_rows), BF16),
            pltpu.VMEM((swaps, 2, LOADS, SLAB_ROWS), BF16),
            pltpu.VMEM((swaps, 2, LOADS, SLAB_ROWS), BF16),
            pltpu.VMEM((solves, n_sub, LOADS, LANES), F32),
            pltpu.VMEM((solves, n_grp, LOADS, coarse + 2 * LANES), BF16),
            dma((n_sub,)), dma((n_sub,)), dma((n_sub,)), dma((n_sub,)), dma((n_grp,)), dma((n_grp,)),
            dma((swaps, n_sub)), dma((swaps, n_sub)), dma((swaps, 2)), dma((swaps, 2)),
            dma((solves, n_sub)), dma((solves, n_sub)), dma((solves, n_grp)), dma((solves, n_grp)),
        ],
        compiler_params=pltpu.CompilerParams(
            collective_id=0, has_side_effects=True, vmem_limit_bytes=48 << 20),
    )(*fetched, dirichlet_ids[0, 0], target, coarse_rows, row_counts[0, 0])
    return (mult[None, None], res[None, None])


def per_device(*args):
    coarse = args[8].shape[1]
    peer_rows = (args[10].shape[2] - 2 * SLAB_ROWS) // lax.axis_size("sub")
    small = coarse * coarse * args[8].dtype.itemsize <= WHOLE_COARSE_BYTES
    aligned = peer_rows % LANES == 0 and coarse % LANES == 0 and args[8].shape[0] % 8 == 0
    aligned = aligned and lax.axis_size("grp") % 2 == 0
    return (fused_device if small and aligned else spread_device)(*args)


def solution(mesh):
    in_specs = (
        P("grp", "sub", None, None),
        P(),
        P("grp", "sub", None, None),
        P("grp", "sub", None, None, None),
        P("grp", "sub", None, None, None),
        P("grp", "sub", None, None, None),
        P("grp", "sub", None, None, None),
        P("grp", "sub", None, None),
        P(("grp", "sub"), None),
        P("grp", "sub", None),
        P("grp", "sub", None),
    )
    out_specs = (P("grp", "sub", None, None), P("grp", "sub", None, None))
    return jax.shard_map(
        per_device, mesh=mesh, in_specs=in_specs, out_specs=out_specs, check_vma=False
    )
```

```python
import jax
import jax.numpy as jnp
from jax import lax
from jax.experimental import pallas as pl
from jax.experimental.pallas import tpu as pltpu
from jax.sharding import PartitionSpec as P
import functools

IFACE = 512
SUBS_DEV = 3
LOADS = 16
CORNERS = 24
SLAB_ROWS = 256
ITERS = 2
LANES = 128
WHOLE_COARSE_BYTES = 4 << 20


def extended(cells, sides, width):
    for axis, dim in sides:
        count = lax.axis_size(axis)
        ends = count - 1
        head = lax.slice_in_dim(cells, 0, width, axis=dim)
        tail = lax.slice_in_dim(cells, cells.shape[dim] - width, cells.shape[dim], axis=dim)
        cells = jnp.concatenate(
            [
                lax.ppermute(tail, axis, [(i, (i + 1) % count) for i in range(ends)]),
                cells,
                lax.ppermute(head, axis, [((i + 1) % count, i) for i in range(ends)]),
            ],
            axis=dim,
        )
    return cells


def spread_device(
    loads,
    boundary_values,
    dirichlet_ids,
    dirichlet_coupling,
    local_inverse,
    local_schur,
    corner_coupling,
    corner_ids,
    coarse_inverse,
    row_counts,
    slot_of,
):
    load_cases = loads[0, 0]
    fixed_ids = dirichlet_ids[0, 0]
    fixed_coupling = dirichlet_coupling[0, 0]
    inverse_blocks = local_inverse[0, 0]
    schur_blocks = local_schur[0, 0]
    coupling = corner_coupling[0, 0]
    corner_index = corner_ids[0, 0].reshape(-1)
    counts = row_counts[0, 0]
    slots = slot_of[0, 0]
    n_sub = lax.axis_size("sub")
    length = slots.shape[0]
    peer_rows = (length - 2 * SLAB_ROWS) // n_sub
    within = n_sub * peer_rows
    coarse_size = coarse_inverse.shape[1]
    positions = jnp.arange(length, dtype=jnp.int32)
    slot_inverse = jnp.zeros(length, jnp.int32).at[slots].set(positions)
    column = jnp.where(
        positions < within, positions // peer_rows, n_sub + (positions - within) // SLAB_ROWS
    )
    offset = jnp.where(positions < within, positions % peer_rows, (positions - within) % SLAB_ROWS)
    canon_live = (offset < counts[column]).astype(jnp.float32)
    live_mask = canon_live[slot_inverse][None, :]
    peer_index = slots[:within].reshape(n_sub, peer_rows)
    slab_index = slots[within:].reshape(2, SLAB_ROWS)
    slab_block = lax.all_to_all(coarse_inverse, "sub", split_axis=1, concat_axis=0, tiled=True)

    def partner(values):
        outgoing = jnp.take(values, peer_index, axis=1)
        incoming = lax.all_to_all(outgoing, "sub", split_axis=1, concat_axis=1, tiled=True).reshape(
            LOADS, within
        )
        slab_part = jnp.take(values, slab_index, axis=1)
        padded = extended(slab_part, (("grp", 1),), 1)
        joined = jnp.concatenate([incoming, padded[:, 0], padded[:, 3]], axis=1)
        return jnp.take(joined, slot_inverse, axis=1)

    def apply_tilde(field_b):
        blocks = field_b.reshape(LOADS, SUBS_DEV, IFACE)
        local_part = jnp.einsum(
            "anm,ram->ran", inverse_blocks, blocks, preferred_element_type=jnp.float32
        )
        corner_terms = jnp.einsum(
            "acm,ram->rac", coupling, blocks, preferred_element_type=jnp.float32
        )
        partial_load = (
            jnp.zeros((LOADS, coarse_size), jnp.float32)
            .at[:, corner_index]
            .add(corner_terms.reshape(LOADS, -1))
        )
        column_load = lax.psum_scatter(partial_load, "sub", scatter_dimension=1, tiled=True)
        column_total = lax.psum(column_load, "grp")
        block_term = jnp.einsum(
            "rj,ij->ri",
            column_total.astype(jnp.bfloat16),
            slab_block,
            preferred_element_type=jnp.float32,
        )
        slab_values = lax.psum(block_term, "sub")
        coarse_values = lax.all_gather(slab_values, "grp", axis=1, tiled=True)
        at_corners = (
            jnp.take(coarse_values, corner_index, axis=1)
            .astype(jnp.bfloat16)
            .reshape(LOADS, SUBS_DEV, CORNERS)
        )
        correction = jnp.einsum(
            "acm,rac->ram", coupling, at_corners, preferred_element_type=jnp.float32
        )
        return (local_part + correction).reshape(LOADS, length)

    def jumps(values):
        return live_mask * (values - partner(values))

    picked = jnp.take(boundary_values, fixed_ids, axis=1).astype(jnp.bfloat16)
    lifted_part = jnp.einsum(
        "and,rad->ran", fixed_coupling, picked, preferred_element_type=jnp.float32
    ).reshape(LOADS, length)
    lifted = live_mask * (load_cases.astype(jnp.float32) - lifted_part)
    jump_field = jumps(apply_tilde(lifted.astype(jnp.bfloat16)))
    multipliers = jnp.zeros_like(jump_field)
    residual = jump_field
    search = jump_field
    inner_before = jnp.ones((LOADS,), jnp.float32)
    for step in range(ITERS):
        smoothed = jnp.einsum(
            "anm,ram->ran",
            schur_blocks,
            residual.astype(jnp.bfloat16).reshape(LOADS, SUBS_DEV, IFACE),
            preferred_element_type=jnp.float32,
        ).reshape(LOADS, length)
        precond = 0.25 * live_mask * (smoothed - partner(smoothed))
        inner_now = lax.psum(jnp.sum(residual * precond, axis=1), ("grp", "sub"))
        if step == 0:
            search = precond
        else:
            search = precond + (inner_now / inner_before)[:, None] * search
        tilde = apply_tilde(search.astype(jnp.bfloat16))
        image = jumps(tilde)
        curvature = lax.psum(jnp.sum(search * image, axis=1), ("grp", "sub"))
        step_size = (inner_now / curvature)[:, None]
        multipliers = multipliers + step_size * search
        residual = residual - step_size * image
        inner_before = inner_now
    return (multipliers[None, None], residual[None, None])


F32 = jnp.float32
BF16 = jnp.bfloat16
MESH = pl.DeviceIdType.MESH
NT = (((1,), (1,)), ((), ()))


def mm(a, b):
    return jnp.dot(a, b, preferred_element_type=F32)


def mm_nt(a, b):
    return lax.dot_general(a, b, NT, preferred_element_type=F32)


def onehot(ids_row, first, rows):
    place = lax.broadcasted_iota(jnp.int32, (rows, ids_row.shape[1]), 0) + first
    return jnp.where(place == ids_row, 1.0, 0.0).astype(BF16)


def fused_kernel(
    n_grp, n_sub, peer_rows, coarse,
    loads_hbm, bound_hbm, fixcpl_hbm, inv_hbm, schur_hbm, cpl_hbm, slots_hbm, fixed_ref, target_ref, cinv_ref,
    counts_ref,
    mult_ref, res_ref,
    loads_ref, bound_ref, fixcpl_ref, inv_ref, schur_ref, cpl_ref, slots_ref, fetched,
    perm, perm_t, cplf, cplb, cinvf, cinvb, place, ids_all, cinv_all, to_peer, from_peer, to_slab, from_slab,
    slab_terms, slab_loads,
    id_send, id_recv, cz_send, cz_recv, cg_send, cg_recv,
    p_send, p_recv, h_send, h_recv, t_send, t_recv, l_send, l_recv,
):
    g = lax.axis_index("grp")
    s = lax.axis_index("sub")
    length = slots_ref.shape[1]
    fetch = {}
    for k, (name, source, held) in enumerate([
        ("bound", bound_hbm, bound_ref), ("fixcpl", fixcpl_hbm, fixcpl_ref), ("slots", slots_hbm, slots_ref),
        ("loads", loads_hbm, loads_ref), ("cpl", cpl_hbm, cpl_ref), ("inv", inv_hbm, inv_ref),
        ("schur", schur_hbm, schur_ref),
    ]):
        fetch[name] = pltpu.make_async_copy(source, held, fetched.at[k])
        fetch[name].start()
    within = n_sub * peer_rows
    corners = SUBS_DEV * CORNERS
    own_rows = coarse // (n_grp * n_sub)

    ids_all[s] = target_ref[...]
    cinv_all[g, s] = cinv_ref[...]
    from_peer[...] = jnp.zeros_like(from_peer)
    from_slab[...] = jnp.zeros_like(from_slab)

    barrier = pltpu.get_barrier_semaphore()
    for k in range(1, n_sub):
        pl.semaphore_signal(barrier, inc=1, device_id=(g, lax.rem(s + k, n_sub)), device_id_type=MESH)
    for k in range(1, n_grp):
        pl.semaphore_signal(barrier, inc=1, device_id=(lax.rem(g + k, n_grp), s), device_id_type=MESH)
    pl.semaphore_wait(barrier, n_sub + n_grp - 2)

    def over_sub(buf_at, send, recv):
        copies = []
        for k in range(1, n_sub):
            copies.append(pltpu.make_async_remote_copy(
                src_ref=buf_at, dst_ref=buf_at, send_sem=send.at[k], recv_sem=recv.at[k],
                device_id=(g, lax.rem(s + k, n_sub)), device_id_type=MESH))
        for copy in copies:
            copy.start()
        return copies

    def over_grp(buf_at, send, recv):
        copies = []
        for k in range(1, n_grp):
            copies.append(pltpu.make_async_remote_copy(
                src_ref=buf_at, dst_ref=buf_at, send_sem=send.at[k], recv_sem=recv.at[k],
                device_id=(lax.rem(g + k, n_grp), s), device_id_type=MESH))
        for copy in copies:
            copy.start()
        return copies

    mate = g + 1 - 2 * lax.rem(g, 2)

    def coarse_rows_to(k, device, block):
        return pltpu.make_async_remote_copy(
            src_ref=cinv_all.at[block], dst_ref=cinv_all.at[block], send_sem=cg_send.at[k], recv_sem=cg_recv.at[k],
            device_id=(device, s), device_id_type=MESH)

    cz_copies = over_sub(cinv_all.at[g, s], cz_send, cz_recv)
    id_copies = over_sub(ids_all.at[s], id_send, id_recv)

    fetch["bound"].wait()
    fetch["fixcpl"].wait()
    bound = bound_ref[...].astype(BF16)
    lifts = []
    for a in range(SUBS_DEV):
        picked = mm(bound, onehot(fixed_ref[a:a + 1, :], 0, bound_ref.shape[1]))
        lifts.append(mm_nt(picked.astype(BF16), fixcpl_ref[a]))
    lift = jnp.concatenate(lifts, axis=1)

    for copy in cz_copies:
        copy.wait()
    cg_direct = [coarse_rows_to(k, lax.rem(g + k, n_grp), g) for k in range(2, n_grp, 2)]
    cg_passed = [coarse_rows_to(k + 1, mate, lax.rem(g + n_grp - k, n_grp)) for k in range(0, n_grp, 2)]
    for copy in cg_direct + cg_passed[:1]:
        copy.start()

    chunk = LANES
    fetch["slots"].wait()

    @pl.loop(0, length // chunk)
    def _(i):
        start = pl.multiple_of(i * chunk, chunk)
        ids = jnp.broadcast_to(slots_ref[:, pl.ds(start, chunk)].astype(F32), (chunk, chunk))
        ids = jnp.transpose(ids).astype(jnp.int32)
        for c in range(length // LANES):
            at = lax.broadcasted_iota(jnp.int32, (chunk, LANES), 1) + c * LANES
            perm_t[pl.ds(start, chunk), c * LANES:(c + 1) * LANES] = jnp.where(at == ids, 1.0, 0.0).astype(BF16)

    column = lax.broadcasted_iota(jnp.int32, (LOADS, length), 1)
    low = jnp.zeros((LOADS, length), jnp.int32)
    count = jnp.zeros((LOADS, length), jnp.int32)
    for p in range(n_sub + 2):
        first = p * peer_rows if p <= n_sub else within + SLAB_ROWS
        low = jnp.where(column >= first, first, low)
        count = jnp.where(column >= first, counts_ref[p], count)
    canon_live = jnp.where(column - low < count, 1.0, 0.0).astype(BF16)
    live = mm(canon_live, perm_t[...])

    fetch["cpl"].wait()
    cplf[...] = jnp.zeros_like(cplf)
    for a in range(SUBS_DEV):
        cplf[a * CORNERS:(a + 1) * CORNERS, a * IFACE:(a + 1) * IFACE] = cpl_ref[a].astype(F32)
    cplb[...] = cplf[...].astype(BF16)

    fetch["loads"].wait()
    lifted = live * (loads_ref[...].astype(F32) - lift)

    def late_tables():
        for copy in id_copies:
            copy.wait()
        for q in range(n_sub):
            place[:, q * LANES:(q + 1) * LANES] = onehot(ids_all[q], 0, coarse + LANES)

        @pl.loop(0, length // chunk)
        def _(i):
            start = pl.multiple_of(i * chunk, chunk)
            perm[pl.ds(start, chunk), :] = onehot(slots_ref[...], start, chunk)

    own_place = onehot(target_ref[...], 0, coarse)

    fetch["inv"].wait()
    fetch["schur"].wait()

    def blocks_apply(ref, field_b):
        return jnp.concatenate(
            [mm(field_b[:, a * IFACE:(a + 1) * IFACE], ref[a]) for a in range(SUBS_DEV)], axis=1)

    lane = lax.broadcasted_iota(jnp.int32, (LOADS, LANES), 1)

    def row_sum(x):
        return jnp.sum(x, axis=1, keepdims=True)

    def tilde(i, field, extra):
        field_b = field.astype(BF16)
        message = mm_nt(field_b, cplb[...])
        local = blocks_apply(inv_ref, field_b) if i > 0 else None
        sums = extra(local)
        for k, part in enumerate(sums):
            message = jnp.where(lane == corners + k, part, message)
        slab_terms[i, s] = message
        term_copies = over_sub(slab_terms.at[i, s], t_send.at[i], t_recv.at[i])
        if i == 0:
            local = blocks_apply(inv_ref, field_b)
            late_tables()
        for copy in term_copies:
            copy.wait()
        terms = jnp.concatenate([slab_terms[i, q] for q in range(n_sub)], axis=1)
        high = terms.astype(BF16)
        rest = (terms - high.astype(F32)).astype(BF16)
        both = mm_nt(jnp.concatenate([high, rest], axis=0), place[...])
        dense = both[:LOADS] + both[LOADS:]
        total = dense[:, coarse:]
        total_high = total.astype(BF16)
        slab_loads[i, g] = jnp.concatenate(
            [dense[:, :coarse].astype(BF16), total_high, (total - total_high.astype(F32)).astype(BF16)], axis=1)
        load_copies = over_grp(slab_loads.at[i, g], l_send.at[i], l_recv.at[i])
        if i == 0:
            for copy, passed in zip(cg_direct, cg_passed[1:]):
                copy.wait()
                passed.start()
        for copy in load_copies:
            copy.wait()
        if i == 0:
            for copy in cg_passed:
                copy.wait()
            for d in range(n_grp * n_sub):
                part = cinv_all[d // n_sub, d % n_sub].astype(F32)
                cinvf[d * own_rows:(d + 1) * own_rows, :] = part[:own_rows]
            cinvb[...] = cinvf[...].astype(BF16)
        whole = slab_loads[i, 0].astype(F32)
        for q in range(1, n_grp):
            whole = whole + slab_loads[i, q].astype(F32)
        load = whole[:, :coarse]
        values = mm(load.astype(BF16), cinvb[...])
        corner_values = mm(values.astype(BF16), own_place)
        result = local + mm(corner_values.astype(BF16), cplb[...])
        scalars = whole[:, coarse:coarse + LANES] + whole[:, coarse + LANES:]
        found = [row_sum(jnp.where(lane == k, scalars, 0.0)) for k in range(len(sums))]
        return result, local, load, values, found

    def partner(i, field):
        out = mm(field.astype(BF16), perm[...]).astype(BF16)
        for q in range(n_sub):
            to_peer[i, q] = out[:, q * peer_rows:(q + 1) * peer_rows]
        for q in range(2):
            to_slab[i, q] = out[:, within + q * SLAB_ROWS:within + (q + 1) * SLAB_ROWS]
        down = pltpu.make_async_remote_copy(
            src_ref=to_slab.at[i, 0], dst_ref=from_slab.at[i, 1], send_sem=h_send.at[i, 0],
            recv_sem=h_recv.at[i, 1], device_id=(jnp.maximum(g - 1, 0), s), device_id_type=MESH)
        up = pltpu.make_async_remote_copy(
            src_ref=to_slab.at[i, 1], dst_ref=from_slab.at[i, 0], send_sem=h_send.at[i, 1],
            recv_sem=h_recv.at[i, 0], device_id=(jnp.minimum(g + 1, n_grp - 1), s), device_id_type=MESH)

        @pl.when(g > 0)
        def _():
            down.start()

        @pl.when(g < n_grp - 1)
        def _():
            up.start()

        copies = []
        for k in range(1, n_sub):
            to = lax.rem(s + k, n_sub)
            copies.append(pltpu.make_async_remote_copy(
                src_ref=to_peer.at[i, to], dst_ref=from_peer.at[i, s], send_sem=p_send.at[i, k],
                recv_sem=p_recv.at[i, k], device_id=(g, to), device_id_type=MESH))
        for copy in copies:
            copy.start()
        for copy in copies:
            copy.wait()

        @pl.when(g > 0)
        def _():
            down.wait_send()
            up.wait_recv()

        @pl.when(g < n_grp - 1)
        def _():
            up.wait_send()
            down.wait_recv()

        joined = jnp.concatenate(
            [from_peer[i, q] for q in range(n_sub)] + [from_slab[i, q] for q in range(2)], axis=1)
        return mm(joined, perm_t[...])

    def smoothed(residual):
        return blocks_apply(schur_ref, residual.astype(BF16))

    image = tilde(0, lifted, lambda local: [])[0]
    residual = live * (image - partner(0, image))

    smooth = smoothed(residual)
    inner_part = 0.5 * row_sum(residual * smooth)
    first = 0.25 * live * (smooth - partner(1, smooth))
    image0, local0, load0, values0, (inner0, energy0) = tilde(
        1, first, lambda local: [inner_part, row_sum(first * local)])
    energy0 = energy0 + row_sum(load0 * values0)
    size0 = inner0 / (2.0 * energy0)
    residual = residual - size0 * (live * (image0 - partner(2, image0)))

    smooth = smoothed(residual)
    inner_part1 = 0.5 * row_sum(residual * smooth)
    second = 0.25 * live * (smooth - partner(3, smooth))
    image1, _, load1, values1, (inner1, energy1, cross) = tilde(
        2, second, lambda local: [inner_part1, row_sum(second * local), row_sum(second * local0)])
    ratio = inner1 / inner0
    energy1 = energy1 + row_sum(load1 * values1)
    cross = cross + row_sum(load1 * values0)
    energy = energy1 + ratio * (2.0 * cross + ratio * energy0)
    size1 = inner1 / (2.0 * energy)
    search = second + ratio * first
    image = image1 + ratio * image0
    mult_ref[...] = size0 * first + size1 * search
    res_ref[...] = residual - size1 * (live * (image - partner(4, image)))


def fused_device(
    loads,
    boundary_values,
    dirichlet_ids,
    dirichlet_coupling,
    local_inverse,
    local_schur,
    corner_coupling,
    corner_ids,
    coarse_inverse,
    row_counts,
    slot_of,
):
    n_grp, n_sub = lax.axis_size("grp"), lax.axis_size("sub")
    length = slot_of.shape[2]
    peer_rows = (length - 2 * SLAB_ROWS) // n_sub
    coarse = coarse_inverse.shape[1]
    corners = SUBS_DEV * CORNERS
    target = jnp.concatenate(
        [corner_ids[0, 0].reshape(1, corners), coarse + jnp.arange(LANES - corners, dtype=jnp.int32)[None]], axis=1)
    rows = coarse_inverse.shape[0]
    held = -(-rows // 16) * 16
    coarse_rows = jnp.pad(coarse_inverse, ((0, held - rows), (0, 0)))
    vmem = pl.BlockSpec(memory_space=pltpu.VMEM)
    hbm = pl.BlockSpec(memory_space=pltpu.HBM)
    smem = pl.BlockSpec(memory_space=pltpu.SMEM)
    swaps, solves = 2 * ITERS + 1, ITERS + 1
    dma = pltpu.SemaphoreType.DMA
    field = jax.ShapeDtypeStruct((LOADS, length), F32)
    fetched = (
        loads[0, 0], boundary_values, dirichlet_coupling[0, 0], local_inverse[0, 0], local_schur[0, 0],
        corner_coupling[0, 0], slot_of[0],
    )
    mult, res = pl.pallas_call(
        functools.partial(fused_kernel, n_grp, n_sub, peer_rows, coarse),
        out_shape=(field, field),
        in_specs=[hbm] * 7 + [vmem] * 3 + [smem],
        out_specs=(vmem, vmem),
        scratch_shapes=[pltpu.VMEM(x.shape, x.dtype) for x in fetched] + [
            dma((len(fetched),)),
            pltpu.VMEM((length, length), BF16),
            pltpu.VMEM((length, length), BF16),
            pltpu.VMEM((LANES, length), F32),
            pltpu.VMEM((LANES, length), BF16),
            pltpu.VMEM((coarse, coarse), F32),
            pltpu.VMEM((coarse, coarse), BF16),
            pltpu.VMEM((coarse + LANES, n_sub * LANES), BF16),
            pltpu.VMEM((n_sub, 1, LANES), jnp.int32),
            pltpu.VMEM((n_grp, n_sub, held, coarse), BF16),
            pltpu.VMEM((swaps, n_sub, LOADS, peer_rows), BF16),
            pltpu.VMEM((swaps, n_sub, LOADS, peer_rows), BF16),
            pltpu.VMEM((swaps, 2, LOADS, SLAB_ROWS), BF16),
            pltpu.VMEM((swaps, 2, LOADS, SLAB_ROWS), BF16),
            pltpu.VMEM((solves, n_sub, LOADS, LANES), F32),
            pltpu.VMEM((solves, n_grp, LOADS, coarse + 2 * LANES), BF16),
            dma((n_sub,)), dma((n_sub,)), dma((n_sub,)), dma((n_sub,)), dma((n_grp,)), dma((n_grp,)),
            dma((swaps, n_sub)), dma((swaps, n_sub)), dma((swaps, 2)), dma((swaps, 2)),
            dma((solves, n_sub)), dma((solves, n_sub)), dma((solves, n_grp)), dma((solves, n_grp)),
        ],
        compiler_params=pltpu.CompilerParams(
            collective_id=0, has_side_effects=True, vmem_limit_bytes=48 << 20),
    )(*fetched, dirichlet_ids[0, 0], target, coarse_rows, row_counts[0, 0])
    return (mult[None, None], res[None, None])


def per_device(*args):
    coarse = args[8].shape[1]
    peer_rows = (args[10].shape[2] - 2 * SLAB_ROWS) // lax.axis_size("sub")
    small = coarse * coarse * args[8].dtype.itemsize <= WHOLE_COARSE_BYTES
    aligned = peer_rows % LANES == 0 and coarse % LANES == 0 and args[8].shape[0] % 8 == 0
    aligned = aligned and lax.axis_size("grp") % 2 == 0
    return (fused_device if small and aligned else spread_device)(*args)


def solution(mesh):
    in_specs = (
        P("grp", "sub", None, None),
        P(),
        P("grp", "sub", None, None),
        P("grp", "sub", None, None, None),
        P("grp", "sub", None, None, None),
        P("grp", "sub", None, None, None),
        P("grp", "sub", None, None, None),
        P("grp", "sub", None, None),
        P(("grp", "sub"), None),
        P("grp", "sub", None),
        P("grp", "sub", None),
    )
    out_specs = (P("grp", "sub", None, None), P("grp", "sub", None, None))
    return jax.shard_map(
        per_device, mesh=mesh, in_specs=in_specs, out_specs=out_specs, check_vma=False
    )
```
